32 devices in a mesh: groups: 2 (over y), gx: 16 (over z, x, core).
Axes of the slice: x: 2, y: 2, z: 4, core: 2. Of those that a mesh axis runs over, the one named last changes fastest.
Arguments:
- tokens: bfloat16 [640, 8192], P('groups', 'gx'), parts along dimension 0, may hold values from -180 to 180, as said below
- norm_gain: bfloat16 [8192], P('gx'), may hold values from 0.25 to 1.75
- gate_weight: bfloat16 [16, 2048, 7168], P('gx'), may hold values from -0.0625 to 0.0625
- up_weight: bfloat16 [16, 2048, 7168], P('gx'), may hold values from -0.0625 to 0.0625
- down_weight: bfloat16 [16, 7168, 2048], P('gx'), may hold values from -0.03125 to 0.03125
Outputs:
- mixed: bfloat16 [640, 8192], P('groups', 'gx'), parts along dimension 0
The draws below stay inside these ranges and needn't reach their ends.
There are 2 independent parts, one for each index of `groups`. The reference program is written for one: setup_inputs(seed, part) draws one part's arguments, and reference() takes and returns one part's arrays. A program takes and returns all parts, laid end to end along the dimension named above; an argument that names none is the same for every part. Nothing has to cross between parts.
Inputs may be any that keep to these rules, and one draw needn't show every extreme that they name: `tokens`: hidden states with scales that differ between rows and between features.
All inputs are finite; a program needn't handle non-finite values.
Results may differ from the reference program's by a relative error of at most 0.0065.
Values may be sent and summed in bfloat16 or wider, within the bound.
A program may use at most 320 MiB of HBM per device.

```python
import math
import jax
import jax.numpy as jnp
from jax import lax

D = 8192
FF = 28672
ROWS = 320
UNIT_SPLIT = 4
FEAT_SPLIT = 4
N_GX = 16


def draw_tokens(key, part):
    key = jax.random.fold_in(key, 11)
    key_row, key_col, key_base = jax.random.split(key, 3)
    row_scale = jnp.exp(jax.random.uniform(key_row, (ROWS, 1), jnp.float32, 0.0, math.log(10.0)))
    position = jnp.arange(D, dtype=jnp.float32)[None, :] / (D - 1)
    col_scale = jnp.exp(jax.random.uniform(key_col, (1, D), jnp.float32, 0.0, math.log(10.0))) * 3.0 ** position
    base = jnp.clip(jax.random.normal(key_base, (ROWS, D), jnp.float32), -6.0, 6.0)
    return (base * row_scale * col_scale * 0.1).astype(jnp.bfloat16)


def block_scale(key, shape, cuts, low, largest):
    def one(dim, blocks):
        draws = jax.random.uniform(jax.random.fold_in(jax.random.fold_in(key, 6), dim), (blocks,), jnp.float32, low / len(cuts), largest / len(cuts))
        return jnp.repeat(jnp.exp(draws), shape[dim] // blocks).reshape((-1,) + (1,) * (len(shape) - dim - 1))

    loudness = one(*cuts[0])
    for cut in cuts[1:]:
        loudness = loudness * one(*cut)
    return loudness


def bell_draw(key, extent, width, most, cuts=(), kind=jnp.bfloat16):
    array = width * jax.random.normal(key, extent, jnp.float32)
    if cuts:
        array = array * block_scale(key, extent, cuts, -0.22, 0.18)
    return jnp.clip(array, -most, most).astype(kind)


def setup_inputs(seed: int = 0, part: int = 0) -> dict:
    streams_of = jax.random.split(jax.random.key(seed), 6)
    part_splits = jax.random.split(jax.random.fold_in(streams_of[5], part), 6)
    return {
        "tokens": draw_tokens(jax.random.fold_in(jax.random.fold_in(streams_of[5], part), 71), part),
        "norm_gain": jnp.clip(1.0 + 0.15 * jax.random.normal(streams_of[1], (D,), jnp.float32), 0.25, 1.75).astype(jnp.bfloat16),
        "gate_weight": bell_draw(streams_of[2], (N_GX, D // FEAT_SPLIT, FF // UNIT_SPLIT), D ** -0.5, 0.0625, ((0, 16),)),
        "up_weight": bell_draw(streams_of[3], (N_GX, D // FEAT_SPLIT, FF // UNIT_SPLIT), D ** -0.5, 0.0625, ((0, 16),)),
        "down_weight": bell_draw(streams_of[4], (N_GX, FF // UNIT_SPLIT, D // FEAT_SPLIT), FF ** -0.5, 0.03125, ((0, 16),)),
    }


epsilon = 1e-05

def reference(tokens, norm_gain, gate_weight, up_weight, down_weight):

    def whole_in(tiles):
        shaped = tiles.reshape(FEAT_SPLIT, UNIT_SPLIT, D // FEAT_SPLIT, FF // UNIT_SPLIT)
        return jnp.transpose(shaped, (0, 2, 1, 3)).reshape(D, FF)
    shaped_down = down_weight.reshape(FEAT_SPLIT, UNIT_SPLIT, FF // UNIT_SPLIT, D // FEAT_SPLIT)
    whole_down = jnp.transpose(shaped_down, (1, 2, 0, 3)).reshape(FF, D)
    widened = tokens.astype(jnp.float32)
    scaling = lax.rsqrt(lax.optimization_barrier(jnp.mean(widened * widened, axis=1, keepdims=True)) + epsilon)
    normed = (widened * scaling * norm_gain.astype(jnp.float32)).astype(jnp.bfloat16)
    gate_value = jnp.dot(normed, whole_in(gate_weight), preferred_element_type=jnp.float32)
    up_value = jnp.dot(normed, whole_in(up_weight), preferred_element_type=jnp.float32)
    hidden = (jax.nn.silu(gate_value) * up_value).astype(jnp.bfloat16)
    return jnp.dot(hidden, whole_down, preferred_element_type=jnp.float32).astype(jnp.bfloat16)
```

```python
import functools

import jax
import jax.numpy as jnp
from jax import lax
from jax.experimental import pallas as pl
from jax.experimental.pallas import tpu as pltpu
from jax.sharding import PartitionSpec as P

epsilon = 1e-05
F32 = jnp.float32
BF16 = jnp.bfloat16

UNIT_CHUNK = 128
LAG = 2
SLOTS = 3
GAIN_ROWS = 16


def slab_kernel(n, feat_split, features, x_ref, gate_ref, up_ref, down_ref, out_ref,
                raw, square_part, square_block, normed, acc, fresh, parts, hidden,
                wide_tile, down_tile, sib_out, sib_in, row_out, row_in,
                raw_send, raw_recv, pass_send, pass_recv, sq_send, sq_recv, sb_send, sb_recv,
                part_send, part_recv, hid_send, hid_recv, wide_sem, down_sem,
                sib_send, sib_recv, row_send, row_recv):
    R = feat_split
    U = n // R
    H = U // 2
    rows = out_ref.shape[0]
    w = out_ref.shape[1]
    units = gate_ref.shape[2]
    CH = UNIT_CHUNK
    K = units // 2 // CH

    me = lax.axis_index("gx")
    r = me // U
    c = me % U
    h = c // 2
    s = c % 2
    base = me - c
    sibling = base + 2 * h + 1 - s

    def at(index):
        return {"gx": index}

    def remote(src, dst, send, recv, target):
        return pltpu.make_async_remote_copy(
            src_ref=src, dst_ref=dst, send_sem=send, recv_sem=recv,
            device_id=at(target), device_id_type=pl.DeviceIdType.MESH)

    def wide_copies(d, k):
        slot = k % SLOTS
        start = pl.multiple_of(d * (units // 2) + k * CH, CH)
        return [
            pltpu.make_async_copy(ref.at[0, :, pl.ds(start, CH)],
                                  wide_tile.at[d, slot, :, pl.ds(i * CH, CH)],
                                  wide_sem.at[d, slot, i])
            for i, ref in enumerate((gate_ref, up_ref))
        ]

    def down_copy(d, k):
        slot = k % SLOTS
        start = pl.multiple_of(d * (units // 2) + k * CH, CH)
        return pltpu.make_async_copy(down_ref.at[0, pl.ds(start, CH), :],
                                     down_tile.at[d, slot], down_sem.at[d, slot])

    for k in range(min(SLOTS, K)):
        for d in range(2):
            for copy in wide_copies(d, k):
                copy.start()
            down_copy(d, k).start()

    barrier = pltpu.get_barrier_semaphore()
    for i in range(1, U):
        pl.semaphore_signal(barrier, inc=1, device_id=at(base + (c + i) % U),
                            device_id_type=pl.DeviceIdType.MESH)
    for i in range(1, R):
        pl.semaphore_signal(barrier, inc=1, device_id=at((me + i * U) % n),
                            device_id_type=pl.DeviceIdType.MESH)
    pl.semaphore_wait(barrier, U - 1 + R - 1)

    def raw_copy(i):
        target = sibling if i == 0 else base + 2 * ((h + i) % H) + s
        return remote(x_ref, raw.at[c], raw_send.at[i], raw_recv.at[i], target)

    def pass_copy(i):
        source = 2 * ((h + H - i) % H) + s
        return remote(raw.at[source], raw.at[source], pass_send.at[i], pass_recv.at[i], sibling)

    for i in range(1, H):
        raw_copy(i).start()
    raw_copy(0).start()

    own = x_ref[:rows, :].astype(F32)
    column = jnp.sum(own * own, axis=1, keepdims=True)
    eye = (lax.broadcasted_iota(jnp.int32, (rows, rows), 0)
           == lax.broadcasted_iota(jnp.int32, (rows, rows), 1))
    square_part[c] = jnp.broadcast_to(
        jnp.sum(jnp.where(eye, column, 0.0), axis=0, keepdims=True), (8, rows))

    def sq_copy(i):
        return remote(square_part.at[c], square_part.at[c], sq_send.at[i], sq_recv.at[i],
                      base + (c + i) % U)

    for i in range(1, U):
        sq_copy(i).start()
    raw[c] = x_ref[...]
    acc[...] = jnp.zeros_like(acc)
    for i in range(1, U):
        sq_copy(i).wait()
    square_block[r] = jnp.sum(square_part[...], axis=0)

    def sb_copy(i):
        return remote(square_block.at[r], square_block.at[r], sb_send.at[i], sb_recv.at[i],
                      (me + i * U) % n)

    for i in range(1, R):
        sb_copy(i).start()
    for i in range(1, R):
        sb_copy(i).wait()
    total = jnp.sum(square_block[...], axis=0)[0:1, :]
    total = jnp.sum(jnp.where(eye, total, 0.0), axis=1, keepdims=True)
    scaling = lax.rsqrt(total / features + epsilon)

    for i in range(1, H):
        raw_copy(i).wait_recv()
        pass_copy(i).start()
    raw_copy(0).wait_recv()
    for i in range(1, H):
        pass_copy(i).wait_recv()
    for j in range(U):
        gain = raw[j, rows:, :].astype(F32)[0:1, :]
        block = raw[j, :rows, :].astype(F32)
        normed[:, j * w:(j + 1) * w] = (block * scaling * gain).astype(BF16)
    for i in range(H):
        raw_copy(i).wait_send()
    for i in range(1, H):
        pass_copy(i).wait_send()

    position = (r, R - 1 - r)
    ahead = ((me + U) % n, (me + n - U) % n)
    behind = ((me + n - U) % n, (me + U) % n)

    def part_copy(d, k):
        return remote(parts.at[d, k], parts.at[d, k], part_send.at[d, k], part_recv.at[d, k],
                      ahead[d])

    def hid_copy(d, k):
        return remote(hidden.at[d, k], hidden.at[d, k], hid_send.at[d, k], hid_recv.at[d, k],
                      behind[d])

    def step(t, carry):
        for d in range(2):
            pos = position[d]
            kh = t - LAG * (R - 1) - LAG * (R - 1 - pos)

            @pl.when((kh >= 0) & (kh < K) & (pos < R - 1))
            def _():
                hid_copy(d, kh).wait_recv()

                @pl.when(pos > 0)
                def _():
                    hid_copy(d, kh).start()

        for d in range(2):
            pos = position[d]
            kp = t - LAG * pos

            @pl.when((kp >= 0) & (kp < K))
            def _():
                for copy in wide_copies(d, kp):
                    copy.wait()
                fresh[d] = jnp.dot(normed[...], wide_tile[d, kp % SLOTS],
                                   preferred_element_type=F32)

                @pl.when(kp + SLOTS < K)
                def _():
                    for copy in wide_copies(d, kp + SLOTS):
                        copy.start()

                @pl.when(pos == 0)
                def _():
                    parts[d, kp] = fresh[d].astype(BF16)

                @pl.when(pos > 0)
                def _():
                    part_copy(d, kp).wait_recv()

                @pl.when((pos > 0) & (pos < R - 1))
                def _():
                    parts[d, kp] = (fresh[d] + parts[d, kp].astype(F32)).astype(BF16)

                @pl.when(pos < R - 1)
                def _():
                    part_copy(d, kp).start()

                @pl.when(pos == R - 1)
                def _():
                    whole = fresh[d] + parts[d, kp].astype(F32)
                    gate = whole[:, :CH]
                    hidden[d, kp] = (gate / (1.0 + jnp.exp(-gate)) * whole[:, CH:]).astype(BF16)
                    hid_copy(d, kp).start()

        for d in range(2):
            pos = position[d]
            kh = t - LAG * (R - 1) - LAG * (R - 1 - pos)

            @pl.when((kh >= 0) & (kh < K))
            def _():
                down_copy(d, kh).wait()
                value = hidden[d, kh]
                for j in range(U):
                    acc[j] += jnp.dot(value, down_tile[d, kh % SLOTS, :, j * w:(j + 1) * w],
                                      preferred_element_type=F32)

                @pl.when(kh + SLOTS < K)
                def _():
                    down_copy(d, kh + SLOTS).start()
        return carry

    lax.fori_loop(0, K + 2 * LAG * (R - 1), step, 0)

    def sib_copy(i):
        other = (h + i) % H
        return remote(sib_out.at[other], sib_in.at[other], sib_send.at[i], sib_recv.at[i], sibling)

    def row_copy(i):
        return remote(row_out.at[i], row_in.at[i], row_send.at[i], row_recv.at[i],
                      base + 2 * ((h + i) % H) + s)

    for i in list(range(1, H)) + [0]:
        other = (h + i) % H
        sib_out[other] = acc[2 * other + 1 - s].astype(BF16)
        sib_copy(i).start()
    for i in range(1, H):
        other = (h + i) % H
        sib_copy(i).wait_recv()
        row_out[i] = (acc[2 * other + s] + sib_in[other].astype(F32)).astype(BF16)
        row_copy(i).start()

    def drain(k, carry):
        for d in range(2):
            pos = position[d]

            @pl.when(pos < R - 1)
            def _():
                part_copy(d, k).wait_send()

            @pl.when(pos > 0)
            def _():
                hid_copy(d, k).wait_send()
        return carry

    lax.fori_loop(0, K, drain, 0)
    sib_copy(0).wait_recv()
    result = acc[2 * h + s] + sib_in[h].astype(F32)
    for i in range(1, H):
        row_copy(i).wait_recv()
        result = result + row_in[i].astype(F32)
    out_ref[...] = result.astype(BF16)
    for i in range(H):
        sib_copy(i).wait_send()
    for i in range(1, H):
        row_copy(i).wait_send()


def per_device(n, tokens, norm_gain, gate_weight, up_weight, down_weight):
    rows, w = tokens.shape
    features = w * n
    feat = gate_weight.shape[1]
    units = gate_weight.shape[2]
    R = features // feat
    U = n // R
    H = U // 2
    K = units // 2 // UNIT_CHUNK
    x = jnp.concatenate([tokens, jnp.broadcast_to(norm_gain[None, :], (GAIN_ROWS, w))], 0)
    dma = pltpu.SemaphoreType.DMA
    vmem = pl.BlockSpec(memory_space=pltpu.VMEM)
    anywhere = pl.BlockSpec(memory_space=pl.ANY)
    return pl.pallas_call(
        functools.partial(slab_kernel, n, R, features),
        out_shape=jax.ShapeDtypeStruct((rows, w), BF16),
        in_specs=[vmem, anywhere, anywhere, anywhere],
        out_specs=vmem,
        scratch_shapes=[
            pltpu.VMEM((U, rows + GAIN_ROWS, w), BF16),
            pltpu.VMEM((U, 8, rows), F32),
            pltpu.VMEM((R, 8, rows), F32),
            pltpu.VMEM((rows, feat), BF16),
            pltpu.VMEM((U, rows, w), F32),
            pltpu.VMEM((2, rows, 2 * UNIT_CHUNK), F32),
            pltpu.VMEM((2, K, rows, 2 * UNIT_CHUNK), BF16),
            pltpu.VMEM((2, K, rows, UNIT_CHUNK), BF16),
            pltpu.VMEM((2, SLOTS, feat, 2 * UNIT_CHUNK), BF16),
            pltpu.VMEM((2, SLOTS, UNIT_CHUNK, feat), BF16),
            pltpu.VMEM((H, rows, w), BF16),
            pltpu.VMEM((H, rows, w), BF16),
            pltpu.VMEM((H, rows, w), BF16),
            pltpu.VMEM((H, rows, w), BF16),
            dma((H,)), dma((H,)), dma((H,)), dma((H,)),
            dma((U,)), dma((U,)), dma((R,)), dma((R,)),
            dma((2, K)), dma((2, K)), dma((2, K)), dma((2, K)),
            dma((2, SLOTS, 2)), dma((2, SLOTS)),
            dma((H,)), dma((H,)), dma((H,)), dma((H,)),
        ],
        compiler_params=pltpu.CompilerParams(
            collective_id=0, has_side_effects=True, vmem_limit_bytes=52 * 2**20),
        cost_estimate=pl.CostEstimate(
            flops=6 * rows * feat * units, bytes_accessed=6 * feat * units,
            transcendentals=rows * units),
    )(x, gate_weight, up_weight, down_weight)


def solution(mesh):
    placed = (
        P("groups", "gx"),
        P("gx"),
        P("gx", None, None),
        P("gx", None, None),
        P("gx", None, None),
    )
    return jax.shard_map(
        functools.partial(per_device, mesh.shape["gx"]),
        mesh=mesh, in_specs=placed, out_specs=P("groups", "gx"), check_vma=False,
    )
```

```python
import functools

import jax
import jax.numpy as jnp
from jax import lax
from jax.experimental import pallas as pl
from jax.experimental.pallas import tpu as pltpu
from jax.sharding import PartitionSpec as P

epsilon = 1e-05
F32 = jnp.float32
BF16 = jnp.bfloat16

UNIT_CHUNK = 256
ROW_SPLIT = 2
LAG = 2
SLOTS = 3
GAIN_ROWS = 16


def chunk_of(units):
    return UNIT_CHUNK if units // 2 % UNIT_CHUNK == 0 else 128


def slab_kernel(n, feat_split, features, x_ref, gate_ref, up_ref, down_ref, out_ref,
                raw, square_part, square_block, scale, normed, acc, fresh, parts, hidden,
                wide_tile, down_tile, sib_out, sib_in, row_out, row_in,
                raw_send, raw_recv, pass_send, pass_recv, sq_send, sq_recv, sb_send, sb_recv,
                part_send, part_recv, hid_send, hid_recv, wide_sem, down_sem,
                sib_send, sib_recv, row_send, row_recv):
    R = feat_split
    U = n // R
    H = U // 2
    Q = ROW_SPLIT
    rows = out_ref.shape[0]
    part = rows // Q
    w = out_ref.shape[1]
    units = gate_ref.shape[2]
    CH = chunk_of(units)
    KU = units // 2 // CH
    K = Q * KU
    T = K + 2 * LAG * (R - 1)

    me = lax.axis_index("gx")
    r = me // U
    c = me % U
    h = c // 2
    s = c % 2
    base = me - c
    sibling = base + 2 * h + 1 - s

    def at(index):
        return {"gx": index}

    def remote(src, dst, send, recv, target):
        return pltpu.make_async_remote_copy(
            src_ref=src, dst_ref=dst, send_sem=send, recv_sem=recv,
            device_id=at(target), device_id_type=pl.DeviceIdType.MESH)

    def wide_copies(d, k):
        slot = k % SLOTS
        start = pl.multiple_of(d * (units // 2) + k % KU * CH, CH)
        return [
            pltpu.make_async_copy(ref.at[0, :, pl.ds(start, CH)],
                                  wide_tile.at[d, slot, :, pl.ds(i * CH, CH)],
                                  wide_sem.at[d, slot, i])
            for i, ref in enumerate((gate_ref, up_ref))
        ]

    def down_copy(d, k):
        slot = k % SLOTS
        start = pl.multiple_of(d * (units // 2) + k % KU * CH, CH)
        return pltpu.make_async_copy(down_ref.at[0, pl.ds(start, CH), :],
                                     down_tile.at[d, slot], down_sem.at[d, slot])

    for k in range(min(SLOTS, K)):
        for d in range(2):
            for copy in wide_copies(d, k):
                copy.start()
            down_copy(d, k).start()

    barrier = pltpu.get_barrier_semaphore()
    for i in range(1, U):
        pl.semaphore_signal(barrier, inc=1, device_id=at(base + (c + i) % U),
                            device_id_type=pl.DeviceIdType.MESH)
    for i in range(1, R):
        pl.semaphore_signal(barrier, inc=1, device_id=at((me + i * U) % n),
                            device_id_type=pl.DeviceIdType.MESH)
    pl.semaphore_wait(barrier, U - 1 + R - 1)

    def raw_copy(q, i):
        target = sibling if i == 0 else base + 2 * ((h + i) % H) + s
        return remote(x_ref.at[q], raw.at[q, c], raw_send.at[q, i], raw_recv.at[q, i], target)

    def pass_copy(q, i):
        source = 2 * ((h + H - i) % H) + s
        return remote(raw.at[q, source], raw.at[q, source], pass_send.at[q, i],
                      pass_recv.at[q, i], sibling)

    def pass_on(q):
        for i in range(1, H):
            raw_copy(q, i).wait_recv()
            pass_copy(q, i).start()

    def normalise(q):
        raw_copy(q, 0).wait_recv()
        for i in range(1, H):
            pass_copy(q, i).wait_recv()
        for j in range(U):
            gain = raw[q, j, part:, :].astype(F32)[0:1, :]
            block = raw[q, j, :part, :].astype(F32)
            normed[q, :, j * w:(j + 1) * w] = (
                block * scale[q * part:(q + 1) * part, :] * gain).astype(BF16)
        for i in range(H):
            raw_copy(q, i).wait_send()
        for i in range(1, H):
            pass_copy(q, i).wait_send()

    for q in range(Q):
        for i in range(1, H):
            raw_copy(q, i).start()
        raw_copy(q, 0).start()

    column = []
    for q in range(Q):
        own = x_ref[q, :part, :].astype(F32)
        column.append(jnp.sum(own * own, axis=1, keepdims=True))
    column = jnp.concatenate(column, axis=0)
    eye = (lax.broadcasted_iota(jnp.int32, (rows, rows), 0)
           == lax.broadcasted_iota(jnp.int32, (rows, rows), 1))
    square_part[c] = jnp.broadcast_to(
        jnp.sum(jnp.where(eye, column, 0.0), axis=0, keepdims=True), (8, rows))

    def sq_copy(i):
        return remote(square_part.at[c], square_part.at[c], sq_send.at[i], sq_recv.at[i],
                      base + (c + i) % U)

    for i in range(1, U):
        sq_copy(i).start()
    for q in range(Q):
        raw[q, c] = x_ref[q]
    acc[...] = jnp.zeros_like(acc)
    for i in range(1, U):
        sq_copy(i).wait()
    square_block[r] = jnp.sum(square_part[...], axis=0)

    def sb_copy(i):
        return remote(square_block.at[r], square_block.at[r], sb_send.at[i], sb_recv.at[i],
                      (me + i * U) % n)

    for i in range(1, R):
        sb_copy(i).start()
    for i in range(1, R):
        sb_copy(i).wait()
    total = jnp.sum(square_block[...], axis=0)[0:1, :]
    total = jnp.sum(jnp.where(eye, total, 0.0), axis=1, keepdims=True)
    scale[...] = lax.rsqrt(total / features + epsilon)
    pass_on(0)
    normalise(0)

    position = (r, R - 1 - r)
    ahead = ((me + U) % n, (me + n - U) % n)
    behind = ((me + n - U) % n, (me + U) % n)

    def part_copy(d, k):
        return remote(parts.at[d, k], parts.at[d, k], part_send.at[d, k], part_recv.at[d, k],
                      ahead[d])

    def hid_copy(d, k):
        return remote(hidden.at[d, k], hidden.at[d, k], hid_send.at[d, k], hid_recv.at[d, k],
                      behind[d])

    def sib_copy(q, i):
        other = (h + i) % H
        return remote(sib_out.at[q, other], sib_in.at[q, other], sib_send.at[q, i],
                      sib_recv.at[q, i], sibling)

    def row_copy(q, i):
        return remote(row_out.at[q, i], row_in.at[q, i], row_send.at[q, i], row_recv.at[q, i],
                      base + 2 * ((h + i) % H) + s)

    def to_sibling(q):
        for i in list(range(1, H)) + [0]:
            other = (h + i) % H
            sib_out[q, other] = acc[q, 2 * other + 1 - s].astype(BF16)
            sib_copy(q, i).start()

    def to_chips(q):
        for i in range(1, H):
            other = (h + i) % H
            sib_copy(q, i).wait_recv()
            row_out[q, i] = (acc[q, 2 * other + s] + sib_in[q, other].astype(F32)).astype(BF16)
            row_copy(q, i).start()

    def finish(q):
        sib_copy(q, 0).wait_recv()
        result = acc[q, 2 * h + s] + sib_in[q, h].astype(F32)
        for i in range(1, H):
            row_copy(q, i).wait_recv()
            result = result + row_in[q, i].astype(F32)
        out_ref[q * part:(q + 1) * part, :] = result.astype(BF16)
        for i in range(H):
            sib_copy(q, i).wait_send()
        for i in range(1, H):
            row_copy(q, i).wait_send()

    def step(t, carry):
        for q in range(1, Q):
            @pl.when(t == q * KU - 6)
            def _():
                pass_on(q)

            @pl.when(t == q * KU - 3)
            def _():
                normalise(q)

            @pl.when(t == q * KU + 2 * LAG * (R - 1))
            def _():
                to_sibling(q - 1)

            @pl.when(t == q * KU + 2 * LAG * (R - 1) + 2)
            def _():
                to_chips(q - 1)

        for d in range(2):
            kp = t - LAG * position[d]

            @pl.when((kp >= 0) & (kp < K))
            def _():
                for copy in wide_copies(d, kp):
                    copy.wait()
                fresh[d] = jnp.dot(normed[kp // KU], wide_tile[d, kp % SLOTS],
                                   preferred_element_type=F32)

                @pl.when(kp + SLOTS < K)
                def _():
                    for copy in wide_copies(d, kp + SLOTS):
                        copy.start()

        for d in range(2):
            pos = position[d]
            kh = t - LAG * (R - 1) - LAG * (R - 1 - pos)
            kp = t - LAG * pos

            @pl.when((kh >= 0) & (kh < K) & (pos < R - 1))
            def _():
                hid_copy(d, kh).wait_recv()

                @pl.when(pos > 0)
                def _():
                    hid_copy(d, kh).start()

            @pl.when((kp >= 0) & (kp < K))
            def _():
                @pl.when(pos == 0)
                def _():
                    parts[d, kp] = fresh[d].astype(BF16)

                @pl.when(pos > 0)
                def _():
                    part_copy(d, kp).wait_recv()

                @pl.when((pos > 0) & (pos < R - 1))
                def _():
                    parts[d, kp] = (fresh[d] + parts[d, kp].astype(F32)).astype(BF16)

                @pl.when(pos < R - 1)
                def _():
                    part_copy(d, kp).start()

                @pl.when(pos == R - 1)
                def _():
                    whole = fresh[d] + parts[d, kp].astype(F32)
                    gate = whole[:, :CH]
                    hidden[d, kp] = (gate / (1.0 + jnp.exp(-gate)) * whole[:, CH:]).astype(BF16)
                    hid_copy(d, kp).start()

        for d in range(2):
            kh = t - LAG * (R - 1) - LAG * (R - 1 - position[d])

            @pl.when((kh >= 0) & (kh < K))
            def _():
                down_copy(d, kh).wait()
                value = hidden[d, kh]
                for j in range(U):
                    acc[kh // KU, j] += jnp.dot(
                        value, down_tile[d, kh % SLOTS, :, j * w:(j + 1) * w],
                        preferred_element_type=F32)

                @pl.when(kh + SLOTS < K)
                def _():
                    down_copy(d, kh + SLOTS).start()
        return carry

    lax.fori_loop(0, T, step, 0)
    to_sibling(Q - 1)
    to_chips(Q - 1)

    def drain(k, carry):
        for d in range(2):
            pos = position[d]

            @pl.when(pos < R - 1)
            def _():
                part_copy(d, k).wait_send()

            @pl.when(pos > 0)
            def _():
                hid_copy(d, k).wait_send()
        return carry

    lax.fori_loop(0, K, drain, 0)
    for q in range(Q):
        finish(q)


def per_device(n, tokens, norm_gain, gate_weight, up_weight, down_weight):
    rows, w = tokens.shape
    features = w * n
    feat = gate_weight.shape[1]
    units = gate_weight.shape[2]
    R = features // feat
    U = n // R
    H = U // 2
    Q = ROW_SPLIT
    part = rows // Q
    CH = chunk_of(units)
    K = Q * (units // 2 // CH)
    x = jnp.concatenate([tokens.reshape(Q, part, w),
                         jnp.broadcast_to(norm_gain[None, None, :], (Q, GAIN_ROWS, w))], 1)
    dma = pltpu.SemaphoreType.DMA
    vmem = pl.BlockSpec(memory_space=pltpu.VMEM)
    anywhere = pl.BlockSpec(memory_space=pl.ANY)
    return pl.pallas_call(
        functools.partial(slab_kernel, n, R, features),
        out_shape=jax.ShapeDtypeStruct((rows, w), BF16),
        in_specs=[vmem, anywhere, anywhere, anywhere],
        out_specs=vmem,
        scratch_shapes=[
            pltpu.VMEM((Q, U, part + GAIN_ROWS, w), BF16),
            pltpu.VMEM((U, 8, rows), F32),
            pltpu.VMEM((R, 8, rows), F32),
            pltpu.VMEM((rows, 1), F32),
            pltpu.VMEM((Q, part, feat), BF16),
            pltpu.VMEM((Q, U, part, w), F32),
            pltpu.VMEM((2, part, 2 * CH), F32),
            pltpu.VMEM((2, K, part, 2 * CH), BF16),
            pltpu.VMEM((2, K, part, CH), BF16),
            pltpu.VMEM((2, SLOTS, feat, 2 * CH), BF16),
            pltpu.VMEM((2, SLOTS, CH, feat), BF16),
            pltpu.VMEM((Q, H, part, w), BF16),
            pltpu.VMEM((Q, H, part, w), BF16),
            pltpu.VMEM((Q, H, part, w), BF16),
            pltpu.VMEM((Q, H, part, w), BF16),
            dma((Q, H)), dma((Q, H)), dma((Q, H)), dma((Q, H)),
            dma((U,)), dma((U,)), dma((R,)), dma((R,)),
            dma((2, K)), dma((2, K)), dma((2, K)), dma((2, K)),
            dma((2, SLOTS, 2)), dma((2, SLOTS)),
            dma((Q, H)), dma((Q, H)), dma((Q, H)), dma((Q, H)),
        ],
        compiler_params=pltpu.CompilerParams(
            collective_id=0, has_side_effects=True, vmem_limit_bytes=52 * 2**20),
        cost_estimate=pl.CostEstimate(
            flops=6 * rows * feat * units, bytes_accessed=6 * feat * units,
            transcendentals=rows * units),
    )(x, gate_weight, up_weight, down_weight)


def solution(mesh):
    placed = (
        P("groups", "gx"),
        P("gx"),
        P("gx", None, None),
        P("gx", None, None),
        P("gx", None, None),
    )
    return jax.shard_map(
        functools.partial(per_device, mesh.shape["gx"]),
        mesh=mesh, in_specs=placed, out_specs=P("groups", "gx"), check_vma=False,
    )
```
